32 devices in a mesh: dp: 4 (over y, x), expert: 8 (over z, core).
Axes of the slice: x: 2, y: 2, z: 4, core: 2. Of those that a mesh axis runs over, the one named last changes fastest.
Arguments:
- hidden_rows: bfloat16 [4096, 2048], P(('dp', 'expert')), may hold values from -6 to 6
- grad_rows: bfloat16 [4096, 7168], P(('dp', 'expert')), may hold values from -0.52734375 to 0.52734375
- gate_prob: float32 [4096], P(('dp', 'expert')), may hold values from 0.02 to 1
- routes: int32 [4096], P(('dp', 'expert')), may hold values from 0 to 7, as said below
Outputs:
- grad_down: bfloat16 [8, 7168, 2048], P('expert', 'dp')
The draws below stay inside these ranges and needn't reach their ends.
Inputs may be any that keep to these rules, and one draw needn't show every extreme that they name: `routes`: among the rows of one device no expert is named more than 48 times; one expert, the same on every device, is named exactly 48 times on every device; every expert is named by some row.
All inputs are finite; a program needn't handle non-finite values.
Results may differ from the reference program's by a relative error of at most 0.0048.
Values may be sent and summed in bfloat16 or wider, within the bound.
No kernel may reach another device: no remote copies, remote signals or barrier semaphores. Data moves between devices by JAX's collectives and lax.ppermute only.
A program may use at most 64 MiB of HBM per device.

```python
import math
import jax
import jax.numpy as jnp
from jax import lax

D = 7168
FW = 2048
ROWS_DEV = 128
EXPERTS = 8
CAP = 48
ROWS = 4096
ROWS_EXP = 512


def draw_routes(key, part):
    blocks = ROWS // ROWS_DEV
    slot_total = EXPERTS * CAP
    others = ROWS_DEV - CAP
    full_expert = jax.random.randint(jax.random.fold_in(key, 11), (), 0, EXPERTS)
    expert_rank = jax.random.permutation(jax.random.fold_in(key, 12), EXPERTS)
    slot_expert = jnp.repeat(jnp.arange(EXPERTS, dtype=jnp.int32), CAP)
    slot_index = jnp.arange(slot_total, dtype=jnp.int32)
    top_score = 1024 + 96 * EXPERTS + 1

    def one_block(block_idx):
        block_key = jax.random.fold_in(key, 100 + block_idx)
        noise = jax.random.randint(jax.random.fold_in(block_key, 1), (slot_total,), 0, 1024)
        score = noise + 96 * expert_rank[slot_expert]
        forced = (block_idx % EXPERTS).astype(jnp.int32)
        score = jnp.where(slot_index == forced * CAP, top_score, score)
        score = jnp.where(slot_expert == full_expert, -1, score)
        distinct = score * slot_total + slot_index
        picked, picked_idx = lax.top_k(distinct, others)
        chosen = slot_expert[picked_idx]
        block_ids = jnp.concatenate([jnp.full((CAP,), full_expert, jnp.int32), chosen.astype(jnp.int32)])
        return jax.random.permutation(jax.random.fold_in(block_key, 2), block_ids)
    return jax.vmap(one_block)(jnp.arange(blocks, dtype=jnp.int32)).reshape(ROWS).astype(jnp.int32)


def spiked(entries, rng, source, target, shards_of, factor):
    owner, partner = [(jnp.arange(entries.shape[position]) // (entries.shape[position] // shards_of)).reshape([-1 if axis == position else 1 for axis in range(entries.ndim)]) for position in (source, target)]
    chosen = jax.random.permutation(rng, shards_of)[partner]
    strong = (owner == chosen) | (owner == (partner + shards_of // 2) % shards_of)
    return jnp.where(strong, factor * entries, entries)


def shard_levels(own_key, dims, cuts, smallest, top_value):
    gain = 1.0
    for position, shards_of in cuts:
        steps = jax.random.uniform(jax.random.fold_in(jax.random.fold_in(own_key, 6), position), (shards_of,), jnp.float32, smallest / len(cuts), top_value / len(cuts))
        gain = gain * jnp.repeat(jnp.exp(steps), dims[position] // shards_of).reshape((-1,) + (1,) * (len(dims) - 1 - position))
    return gain


def centred(rng, extent, spread, most, cuts=(), kind=jnp.bfloat16):
    gain = shard_levels(rng, extent, cuts, -0.22, 0.18) if cuts else 1.0
    result = jax.random.normal(rng, extent, jnp.float32) * spread * gain
    return jnp.minimum(jnp.maximum(result, -most), most).astype(kind)


def bell_draw_with(rng, dims, deviation, most, shards, heavy, kind=jnp.bfloat16):
    values = deviation * jax.random.normal(rng, dims, jnp.float32)
    if shards:
        values = values * shard_levels(rng, dims, shards, -0.22, 0.18)
    return jnp.clip(spiked(values, jax.random.fold_in(rng, 3), *heavy), -most, most).astype(kind)


def setup_inputs(seed: int = 0) -> dict:
    key_of = jax.random.split(jax.random.key(seed), 5)
    hidden_rows = centred(key_of[0], (ROWS, FW), 1.0, 6.0, ((0, 32),))
    grad_rows = bell_draw_with(key_of[1], (ROWS, D), (2.0 / ROWS_EXP ** 0.5), 0.52734375, ((0, 32),), (0, 1, 32, 2.75))
    gate_prob = jnp.clip(jnp.exp(math.log(1.0) - 3.912023 * jax.random.uniform(key_of[2], (ROWS,), jnp.float32) ** shard_levels(key_of[2], (ROWS,), ((0, 32),), -0.2, 0.2)), 0.02, 1.0)
    routes = draw_routes(jax.random.fold_in(key_of[4], 71), 0)
    return dict(hidden_rows=hidden_rows, grad_rows=grad_rows, gate_prob=gate_prob, routes=routes)


row_block = 512


def reference(hidden_rows, grad_rows, gate_prob, routes):
    weighted = (gate_prob[:, None] * hidden_rows.astype(jnp.float32)).astype(jnp.bfloat16)
    sort_order = jnp.argsort(routes, stable=True).astype(jnp.int32)
    member = (routes[:, None] == jnp.arange(EXPERTS, dtype=jnp.int32)[None, :]).astype(jnp.int32)
    counts = jnp.sum(member, axis=0).astype(jnp.int32)
    starts = (jnp.cumsum(counts) - counts).astype(jnp.int32)
    padded_weighted = jnp.concatenate([weighted[sort_order], jnp.zeros((row_block, FW), weighted.dtype)], axis=0)
    padded_grad = jnp.concatenate([grad_rows[sort_order], jnp.zeros((row_block, D), grad_rows.dtype)], axis=0)

    def per_expert(expert):
        first_row = starts[expert]
        row_total = counts[expert]
        block_count = (row_total + (row_block - 1)) // row_block

        def add_block(index, total):
            begin = (first_row + index * row_block).astype(jnp.int32)
            wpiece = lax.dynamic_slice_in_dim(padded_weighted, begin, row_block, 0)
            gpiece = lax.dynamic_slice_in_dim(padded_grad, begin, row_block, 0)
            keep_rows = (index * row_block + jnp.arange(row_block, dtype=jnp.int32)) < row_total
            wpiece = jnp.where(keep_rows[:, None], wpiece, jnp.zeros((), wpiece.dtype))
            return total + jnp.dot(gpiece.T, wpiece, preferred_element_type=jnp.float32)

        total = lax.fori_loop(jnp.int32(0), block_count.astype(jnp.int32), add_block, jnp.zeros((D, FW), jnp.float32))
        return total.astype(jnp.bfloat16)

    return lax.map(per_expert, jnp.arange(EXPERTS, dtype=jnp.int32))
```

```python
import jax
import jax.numpy as jnp
from jax import lax
from jax.sharding import Mesh, PartitionSpec as P

CORES = 2
ADAPTIVE_CHIPS = 4
STEPS = ((19, 13), (20, 10))


def shifted(value, axis, count):
    return [value] + [
        lax.ppermute(value, axis, [(a, (a + s) % count) for a in range(count)]) for s in range(1, count)
    ]


def spread_columns(value, count):
    width = value.shape[1] // count
    me = lax.axis_index("dp")
    out = []
    for s in range(count):
        block = lax.dynamic_slice_in_dim(value, ((me + s) % count) * width, width, 1)
        if s:
            block = lax.ppermute(block, "dp", [(a, (a + s) % count) for a in range(count)])
        out.append(block)
    return jnp.concatenate(out, axis=0)


def pick(slots, total, rows):
    onehot = (slots[None, :] == jnp.arange(total, dtype=jnp.int32)[:, None]).astype(jnp.bfloat16)
    return jnp.dot(onehot, rows, preferred_element_type=jnp.float32).astype(jnp.bfloat16)


def per_device(hidden_rows, grad_rows, gate_prob, routes):
    row_count = routes.shape[0]
    dp_count = lax.axis_size("dp")
    chips = lax.axis_size("chip")
    experts = chips * CORES
    cap = 3 * row_count * dp_count // experts
    me_dp = lax.axis_index("dp")
    me_chip = lax.axis_index("chip")
    me_core = lax.axis_index("core")

    route_blocks = shifted(routes, "dp", dp_count)
    weighted = (gate_prob[:, None] * hidden_rows.astype(jnp.float32)).astype(jnp.bfloat16)
    hidden_group = spread_columns(weighted, dp_count)

    route_group = jnp.stack(route_blocks)
    source = (me_dp - jnp.arange(dp_count, dtype=jnp.int32)) % dp_count
    member = (route_group[:, :, None] == jnp.arange(experts, dtype=jnp.int32)).astype(jnp.float32)
    below = jnp.tril(jnp.ones((row_count, row_count), jnp.float32), -1)
    inside = jnp.einsum("qr,sre->sqe", below, member, preferred_element_type=jnp.float32)
    block_sum = jnp.sum(member, axis=1)
    before = jnp.einsum(
        "st,te->se", (source[None, :] < source[:, None]).astype(jnp.float32), block_sum
    )
    total = jnp.sum(block_sum, axis=0)
    pair_first = jnp.where(
        jnp.arange(experts) % CORES == 1, jnp.concatenate([jnp.zeros((1,), jnp.float32), total[:-1]]), 0.0
    )
    position = jnp.sum(member * (inside + before[:, None, :] + pair_first), axis=2)
    position = position.astype(jnp.int32).reshape(-1)
    to_chip = route_group.reshape(-1) // CORES
    total = total.astype(jnp.int32)

    both = jnp.stack(shifted(total, "core", CORES))
    counts = jnp.stack(shifted(both, "chip", chips), axis=1)
    chip_counts = counts.reshape(CORES * chips, chips, CORES).sum(-1).max(0)
    mine = lax.dynamic_slice_in_dim(counts, me_chip * CORES, CORES, 2)

    def finish(hidden_full, grad_full, width):
        first = mine[0, :, 0]
        count = jnp.where(me_core == 0, mine[0, :, 0], mine[0, :, 1])
        slots = jnp.arange(width, dtype=jnp.int32)
        own_pos = slots[None, :] - jnp.where(me_core == 0, 0, first)[:, None]
        other_pos = slots[None, :] - jnp.where(me_core == 0, first, 0)[:, None]
        other_count = mine[0, :, 0] + mine[0, :, 1] - count
        window = min(cap, width)

        def target(pos, limit):
            good = (pos >= 0) & (pos < limit[:, None])
            return jnp.where(good, pos, -1)

        own_t = target(own_pos, count)
        other_t = target(other_pos, other_count)
        lanes = jnp.arange(window, dtype=jnp.int32)[None, :, None]
        own_hot = (own_t[:, None, :] == lanes).astype(jnp.bfloat16)
        other_hot = (other_t[:, None, :] == lanes).astype(jnp.bfloat16)

        def windows(full):
            full = full.reshape(chips, width, full.shape[-1])
            own = jnp.einsum("swk,skc->swc", own_hot, full, preferred_element_type=jnp.float32)
            other = jnp.einsum("swk,skc->swc", other_hot, full, preferred_element_type=jnp.float32)
            own = own.astype(jnp.bfloat16).reshape(chips * window, -1)
            other = other.astype(jnp.bfloat16).reshape(chips * window, -1)
            got = lax.ppermute(other, "core", [(a, (a + 1) % CORES) for a in range(CORES)])
            return jnp.concatenate([own, got], axis=0)

        blocks = shifted(hidden_full, "dp", dp_count)
        order = jnp.stack([blocks[0]] + blocks[1:])
        back = (me_dp - jnp.arange(dp_count)) % dp_count
        hidden_wide = jnp.concatenate(
            [lax.dynamic_index_in_dim(order, back[i], 0, keepdims=False) for i in range(dp_count)], axis=1
        )
        return lax.dot_general(
            windows(grad_full), windows(hidden_wide), (((0,), (0,)), ((), ())), preferred_element_type=jnp.float32
        ).astype(jnp.bfloat16)

    def uniform(width):
        def run(grad_rows, hidden_group):
            slots = jnp.where(position < width, to_chip * width + position, -1)

            def send(rows):
                packed = pick(slots, chips * width, rows)
                got = lax.all_to_all(packed, "chip", split_axis=0, concat_axis=0, tiled=True)
                back = (me_chip - jnp.arange(chips)) % chips
                return jnp.take(got.reshape(chips, width, -1), back, axis=0).reshape(chips * width, -1)

            return finish(send(hidden_group), send(spread_columns(grad_rows, dp_count)), width)

        return run

    def uneven(hot, wide, narrow):
        def run(grad_rows, hidden_group):
            ahead = (to_chip - me_chip) % chips
            slots = jnp.where(position < narrow, ahead * narrow + position, -1)
            extra = (to_chip == hot) & (position >= narrow)
            slots = jnp.where(extra, chips * narrow + position - narrow, slots)

            def send(rows):
                packed = pick(slots, chips * narrow + wide - narrow, rows)
                rest = packed[chips * narrow :]
                out = []
                for s in range(chips):
                    block = packed[s * narrow : (s + 1) * narrow]
                    more = rest
                    if s:
                        block = lax.ppermute(block, "chip", [(a, (a + s) % chips) for a in range(chips)])
                        more = lax.ppermute(rest, "chip", [((hot - s) % chips, hot)])
                    out += [block, more]
                return jnp.concatenate(out, axis=0)

            return finish(send(hidden_group), send(spread_columns(grad_rows, dp_count)), wide)

        return run

    if chips > ADAPTIVE_CHIPS:
        return uniform(CORES * cap)(grad_rows, hidden_group)[None]
    hot = jnp.argmax(chip_counts).astype(jnp.int32)
    most = jnp.max(chip_counts)
    others = jnp.max(jnp.where(jnp.arange(chips) == hot, 0, chip_counts))
    branches = [uniform(CORES * cap)]
    which = jnp.int32(0)
    for n, (wide, narrow) in reversed(list(enumerate(STEPS))):
        wide, narrow = wide * cap // 12, narrow * cap // 12
        which = jnp.where((most <= wide) & (others <= narrow), 1 + n * chips + hot, which)
    for wide, narrow in STEPS:
        branches += [uneven(h, wide * cap // 12, narrow * cap // 12) for h in range(chips)]
    return lax.switch(which, branches, grad_rows, hidden_group)[None]


def solution(mesh):
    dp_count, exp_count = mesh.shape["dp"], mesh.shape["expert"]
    fine = Mesh(mesh.devices.reshape(dp_count, exp_count // CORES, CORES), ("dp", "chip", "core"))
    rows = ("dp", "chip", "core")
    placed = (P(rows, None), P(rows, None), P(rows), P(rows))
    return jax.shard_map(
        per_device, mesh=fine, in_specs=placed, out_specs=P(("chip", "core"), "dp", None), check_vma=False
    )
```

```python
import functools

import jax
import jax.numpy as jnp
from jax import lax
from jax.experimental import pallas as pl
from jax.experimental.pallas import tpu as pltpu
from jax.sharding import Mesh, PartitionSpec as P

CORES = 2
ADAPTIVE_CHIPS = 4
UNITS = 12
SIZES = (13, 16, 18, 20, 24)
COLUMN = 256
LAST = 2
VMEM = 48 * 2**20
NO_COST = pl.CostEstimate(flops=0, bytes_accessed=0, transcendentals=0)


def shifted(value, axis, count):
    return [value] + [
        lax.ppermute(value, axis, [(a, (a + s) % count) for a in range(count)]) for s in range(1, count)
    ]


def spread_columns(value, count):
    width = value.shape[1] // count
    me = lax.axis_index("dp")
    out = []
    for s in range(count):
        block = lax.dynamic_slice_in_dim(value, ((me + s) % count) * width, width, 1)
        if s:
            block = lax.ppermute(block, "dp", [(a, (a + s) % count) for a in range(count)])
        out.append(block)
    return jnp.concatenate(out, axis=0)


def pack_kernel(where, *refs):
    chip = pl.program_id(0)
    half = len(refs) // 2
    size = refs[-1].shape[1]
    slot = lax.broadcasted_iota(jnp.int32, (size, where.shape[1]), 0)
    onehot = ((where[1:2, :] == slot) & (where[0:1, :] == chip)).astype(jnp.bfloat16)
    for rows, out in zip(refs[:half], refs[half:]):
        out[0] = jnp.dot(onehot, rows[...], preferred_element_type=jnp.float32).astype(out.dtype)


def pack(where, chips, size, *values):
    count = values[0].shape[0]
    return pl.pallas_call(
        pack_kernel,
        grid=(chips,),
        in_specs=[pl.BlockSpec((2, count), lambda z: (0, 0))]
        + [pl.BlockSpec(v.shape, lambda z: (0, 0)) for v in values],
        out_specs=[pl.BlockSpec((1, size, v.shape[1]), lambda z: (z, 0, 0)) for v in values],
        out_shape=[jax.ShapeDtypeStruct((chips, size, v.shape[1]), jnp.bfloat16) for v in values],
        compiler_params=pltpu.CompilerParams(vmem_limit_bytes=VMEM),
        cost_estimate=pl.CostEstimate(
            flops=2 * chips * size * sum(v.size for v in values),
            bytes_accessed=2 * sum(v.size + chips * size * v.shape[1] for v in values),
            transcendentals=0,
        ),
    )(where, *values)


def exchange(blocks):
    return lax.all_to_all(blocks, "chip", split_axis=0, concat_axis=0, tiled=True)


def plan_kernel(sizes, place, counts, out):
    chips, cores, experts = counts.shape
    chip, core = place[0], place[1]
    for source in range(chips):
        back = lax.rem(chip - source + chips, chips)
        first = counts[back, 0, CORES * chip]
        second = counts[back, 0, CORES * chip + 1]
        out[0, source] = jnp.where(core == 0, 0, first)
        out[1, source] = jnp.where(core == 0, first, second)
        out[2, source] = jnp.where(core == 0, first, 0)
        out[3, source] = jnp.where(core == 0, second, first)
        out[4, source] = 0
    if len(sizes) == 1:
        return
    most = jnp.int32(0)
    for z in range(chips):
        for b in range(chips):
            for c in range(cores):
                most = jnp.maximum(most, counts[b, c, CORES * z] + counts[b, c, CORES * z + 1])
    which = jnp.int32(0)
    for size in sizes[:-1]:
        which += (most > size).astype(jnp.int32)
    out[4, 0] = which


def make_plan(sizes, place, counts):
    smem = pl.BlockSpec(memory_space=pltpu.SMEM)
    return pl.pallas_call(
        functools.partial(plan_kernel, sizes),
        in_specs=[smem, smem],
        out_specs=smem,
        out_shape=jax.ShapeDtypeStruct((5, counts.shape[0]), jnp.int32),
    )(place, counts)


def unpack_kernel(cap, plan, columns, *refs):
    refs, (own, other) = refs[:-2], refs[-2:]
    source = pl.program_id(0)
    wide = own.shape[1] // len(refs)
    shape = (2 * cap, refs[0].shape[1])
    lane = lax.broadcasted_iota(jnp.int32, shape, 0)
    slot = lax.broadcasted_iota(jnp.int32, shape, 1)
    top = lane < cap
    low = jnp.where(top, plan[0, source], plan[2, source] - cap)
    count = jnp.where(top, plan[1, source], plan[3, source] + cap)
    hot = ((slot == lane + low) & (lane < count)).astype(jnp.bfloat16)
    for g, ref in enumerate(refs):
        both = jnp.dot(hot, ref[0], preferred_element_type=jnp.float32).astype(own.dtype)
        at = pl.ds(pl.multiple_of(columns[g] * wide, wide) if len(refs) > 1 else 0, wide)
        own[:, at] = both[:cap]
        other[:, at] = both[cap:]


def unpack(plan, columns, cap, blocks):
    chips, _, wide = blocks[0].shape
    result = jax.ShapeDtypeStruct((chips * cap, wide * len(blocks)), jnp.bfloat16)
    return pl.pallas_call(
        functools.partial(unpack_kernel, cap),
        grid_spec=pltpu.PrefetchScalarGridSpec(
            num_scalar_prefetch=2,
            grid=(chips,),
            in_specs=[pl.BlockSpec((1,) + b.shape[1:], lambda s, *_: (s, 0, 0)) for b in blocks],
            out_specs=[pl.BlockSpec((cap, wide * len(blocks)), lambda s, *_: (s, 0))] * 2,
        ),
        out_shape=[result] * 2,
        compiler_params=pltpu.CompilerParams(vmem_limit_bytes=VMEM),
        cost_estimate=NO_COST,
    )(plan, columns, *blocks)


def product_kernel(*refs):
    grad_a, grad_b, hidden_a, hidden_b, out = refs[-5:]
    wide = 512 if out.shape[1] % 512 == 0 else out.shape[1]
    over_rows = (((0,), (0,)), ((), ()))

    for n in range(0, out.shape[1], wide):
        at = slice(n, n + wide)
        half = lax.dot_general(grad_a[...], hidden_a[:, at], over_rows, preferred_element_type=jnp.float32)
        rest = lax.dot_general(grad_b[...], hidden_b[:, at], over_rows, preferred_element_type=jnp.float32)
        out[:, at] = (half + rest).astype(out.dtype)


def product_into(total, grads, hiddens, first, rows):
    depth, part = grads[0].shape
    wide = hiddens[0].shape[1]
    start = first // COLUMN
    held = [] if total is None else [total]
    return pl.pallas_call(
        product_kernel,
        grid=(part // COLUMN,),
        in_specs=[pl.BlockSpec(memory_space=pl.ANY)] * len(held)
        + [pl.BlockSpec((depth, COLUMN), lambda m: (0, m))] * 2
        + [pl.BlockSpec((depth, wide), lambda m: (0, 0))] * 2,
        out_specs=pl.BlockSpec((COLUMN, wide), lambda m: (m + start, 0)),
        out_shape=jax.ShapeDtypeStruct((rows, wide), jnp.bfloat16),
        input_output_aliases={0: 0} if held else {},
        compiler_params=pltpu.CompilerParams(vmem_limit_bytes=VMEM),
        cost_estimate=NO_COST,
    )(*held, *grads, *hiddens)


def per_device(hidden_rows, grad_rows, gate_prob, routes):
    row_count = routes.shape[0]
    dp_count = lax.axis_size("dp")
    chips = lax.axis_size("chip")
    experts = chips * CORES
    cap = 3 * row_count * dp_count // experts
    width = CORES * cap
    me_dp = lax.axis_index("dp")
    me_chip = lax.axis_index("chip")
    me_core = lax.axis_index("core")
    col_width = grad_rows.shape[1] // dp_count
    blocks = col_width // COLUMN
    cuts = (0, max(1, blocks - LAST) * COLUMN, col_width)

    route_group = jnp.stack(shifted(routes, "dp", dp_count))
    weighted = (gate_prob[:, None] * hidden_rows.astype(jnp.float32)).astype(jnp.bfloat16)
    hidden_group = spread_columns(weighted, dp_count)
    source = ((me_dp - jnp.arange(dp_count)) % dp_count).astype(jnp.int32)
    member = (route_group[:, :, None] == jnp.arange(experts, dtype=jnp.int32)).astype(jnp.float32)
    below = jnp.tril(jnp.ones((row_count, row_count), jnp.float32), -1)
    inside = jnp.einsum("qr,sre->sqe", below, member, preferred_element_type=jnp.float32)
    block_sum = jnp.sum(member, axis=1)
    before = jnp.einsum(
        "st,te->se", (source[None, :] < source[:, None]).astype(jnp.float32), block_sum
    )
    total = jnp.sum(block_sum, axis=0)
    pair_first = jnp.where(
        jnp.arange(experts) % CORES == 1, jnp.concatenate([jnp.zeros((1,), jnp.float32), total[:-1]]), 0.0
    )
    position = jnp.sum(member * (inside + before[:, None, :] + pair_first), axis=2)
    position = position.astype(jnp.int32).reshape(-1)
    to_chip = route_group.reshape(-1) // CORES

    both = jnp.stack(shifted(total.astype(jnp.int32), "core", CORES))
    counts = jnp.stack(shifted(both, "chip", chips))
    units = SIZES if chips <= ADAPTIVE_CHIPS else SIZES[-1:]
    sizes = [size * cap // UNITS for size in units]
    plan = make_plan(sizes, jnp.stack([me_chip, me_core]).astype(jnp.int32), counts)
    where = jnp.stack([to_chip, position])
    early = sizes[-2] if len(sizes) > 1 else sizes[-1]
    hidden_early = pack(where, chips, early, hidden_group)[0]

    def windows(blocks):
        own, other = unpack(plan, source, cap, blocks)
        return own, lax.ppermute(other, "core", [(a, (a + 1) % CORES) for a in range(CORES)])

    def branch(size):
        def run(hidden_early, hidden_group, grad_rows):
            if size <= early:
                hidden_own = hidden_early[:, :size]
            else:
                hidden_own = pack(where, chips, size, hidden_group)[0]
            hidden_own = exchange(hidden_own)
            grad_group = spread_columns(grad_rows, dp_count)
            grad_parts = [grad_group[:, low:high] for low, high in zip(cuts, cuts[1:])]
            packed = lax.optimization_barrier(pack(where, chips, size, *grad_parts))
            hidden_all = shifted(hidden_own, "dp", dp_count)
            parts = [exchange(part) for part in packed]
            hiddens = windows(hidden_all)
            total = None
            for low, part in zip(cuts, parts):
                if total is not None:
                    part, total = lax.optimization_barrier((part, total))
                total = product_into(total, windows([part]), hiddens, low, col_width)
            return total

        return run

    operands = (hidden_early, hidden_group, grad_rows)
    if len(sizes) == 1:
        return branch(sizes[0])(*operands)[None]
    return lax.switch(plan[4, 0], [branch(size) for size in sizes], *operands)[None]


def solution(mesh):
    dp_count, exp_count = mesh.shape["dp"], mesh.shape["expert"]
    fine = Mesh(mesh.devices.reshape(dp_count, exp_count // CORES, CORES), ("dp", "chip", "core"))
    rows = ("dp", "chip", "core")
    placed = (P(rows, None), P(rows, None), P(rows), P(rows))
    return jax.shard_map(
        per_device, mesh=fine, in_specs=placed, out_specs=P(("chip", "core"), "dp", None), check_vma=False
    )
```

```python
import functools

import jax
import jax.numpy as jnp
from jax import lax
from jax.experimental import pallas as pl
from jax.experimental.pallas import tpu as pltpu
from jax.sharding import Mesh, PartitionSpec as P

CORES = 2
ADAPTIVE_CHIPS = 4
UNITS = 12
SIZES = (13, 16, 18, 20, 24)
COLUMN = 256
LAST = 2
VMEM = 48 * 2**20
NO_COST = pl.CostEstimate(flops=0, bytes_accessed=0, transcendentals=0)


def shifted(value, axis, count):
    return [value] + [
        lax.ppermute(value, axis, [(a, (a + s) % count) for a in range(count)]) for s in range(1, count)
    ]


def spread_columns(value, count):
    width = value.shape[1] // count
    me = lax.axis_index("dp")
    out = []
    for s in range(count):
        block = lax.dynamic_slice_in_dim(value, ((me + s) % count) * width, width, 1)
        if s:
            block = lax.ppermute(block, "dp", [(a, (a + s) % count) for a in range(count)])
        out.append(block)
    return jnp.concatenate(out, axis=0)


def pack_kernel(where, *refs):
    chip = pl.program_id(0)
    half = len(refs) // 2
    size = refs[-1].shape[1]
    slot = lax.broadcasted_iota(jnp.int32, (size, where.shape[1]), 0)
    onehot = ((where[1:2, :] == slot) & (where[0:1, :] == chip)).astype(jnp.bfloat16)
    for rows, out in zip(refs[:half], refs[half:]):
        out[0] = jnp.dot(onehot, rows[...], preferred_element_type=jnp.float32).astype(out.dtype)


def pack(where, chips, size, *values):
    count = values[0].shape[0]
    return pl.pallas_call(
        pack_kernel,
        grid=(chips,),
        in_specs=[pl.BlockSpec((2, count), lambda z: (0, 0))]
        + [pl.BlockSpec(v.shape, lambda z: (0, 0)) for v in values],
        out_specs=[pl.BlockSpec((1, size, v.shape[1]), lambda z: (z, 0, 0)) for v in values],
        out_shape=[jax.ShapeDtypeStruct((chips, size, v.shape[1]), jnp.bfloat16) for v in values],
        compiler_params=pltpu.CompilerParams(vmem_limit_bytes=VMEM),
        cost_estimate=pl.CostEstimate(
            flops=2 * chips * size * sum(v.size for v in values),
            bytes_accessed=2 * sum(v.size + chips * size * v.shape[1] for v in values),
            transcendentals=0,
        ),
    )(where, *values)


def exchange(blocks):
    return lax.all_to_all(blocks, "chip", split_axis=0, concat_axis=0, tiled=True)


def plan_kernel(sizes, place, counts, out):
    chips, cores, experts = counts.shape
    chip, core = place[0], place[1]
    for source in range(chips):
        back = lax.rem(chip - source + chips, chips)
        first = counts[back, 0, CORES * chip]
        second = counts[back, 0, CORES * chip + 1]
        out[0, source] = jnp.where(core == 0, 0, first)
        out[1, source] = jnp.where(core == 0, first, second)
        out[2, source] = jnp.where(core == 0, first, 0)
        out[3, source] = jnp.where(core == 0, second, first)
        first = counts[back, 1, CORES * chip]
        second = counts[back, 1, CORES * chip + 1]
        out[4, source] = jnp.where(core == 0, 0, first)
        out[5, source] = jnp.where(core == 0, first, second)
        out[6, source] = 0
    if len(sizes) == 1:
        return
    most = jnp.int32(0)
    for z in range(chips):
        for b in range(chips):
            for c in range(cores):
                most = jnp.maximum(most, counts[b, c, CORES * z] + counts[b, c, CORES * z + 1])
    which = jnp.int32(0)
    for size in sizes[:-1]:
        which += (most > size).astype(jnp.int32)
    out[6, 0] = which


def make_plan(sizes, place, counts):
    smem = pl.BlockSpec(memory_space=pltpu.SMEM)
    return pl.pallas_call(
        functools.partial(plan_kernel, sizes),
        in_specs=[smem, smem],
        out_specs=smem,
        out_shape=jax.ShapeDtypeStruct((7, counts.shape[0]), jnp.int32),
    )(place, counts)


def unpack_kernel(cap, plan, columns, *refs):
    refs, (own, other) = refs[:-2], refs[-2:]
    source = pl.program_id(0)
    wide = own.shape[1] // len(refs)
    shape = (2 * cap, refs[0].shape[1])
    lane = lax.broadcasted_iota(jnp.int32, shape, 0)
    slot = lax.broadcasted_iota(jnp.int32, shape, 1)
    top = lane < cap
    low = jnp.where(top, plan[0, source], plan[2, source] - cap)
    count = jnp.where(top, plan[1, source], plan[3, source] + cap)
    hot = ((slot == lane + low) & (lane < count)).astype(jnp.bfloat16)
    for g, ref in enumerate(refs):
        both = jnp.dot(hot, ref[0], preferred_element_type=jnp.float32).astype(own.dtype)
        at = pl.ds(pl.multiple_of(columns[g] * wide, wide) if len(refs) > 1 else 0, wide)
        own[:, at] = both[:cap]
        other[:, at] = both[cap:]


def unpack(plan, columns, cap, blocks):
    chips, _, wide = blocks[0].shape
    result = jax.ShapeDtypeStruct((chips * cap, wide * len(blocks)), jnp.bfloat16)
    return pl.pallas_call(
        functools.partial(unpack_kernel, cap),
        grid_spec=pltpu.PrefetchScalarGridSpec(
            num_scalar_prefetch=2,
            grid=(chips,),
            in_specs=[pl.BlockSpec((1,) + b.shape[1:], lambda s, *_: (s, 0, 0)) for b in blocks],
            out_specs=[pl.BlockSpec((cap, wide * len(blocks)), lambda s, *_: (s, 0))] * 2,
        ),
        out_shape=[result] * 2,
        compiler_params=pltpu.CompilerParams(vmem_limit_bytes=VMEM),
        cost_estimate=NO_COST,
    )(plan, columns, *blocks)


def select_kernel(cap, plan, own, got, own_out, got_out):
    source = pl.program_id(0)
    shape = (cap, own.shape[1])
    lane = lax.broadcasted_iota(jnp.int32, shape, 0)
    slot = lax.broadcasted_iota(jnp.int32, shape, 1)
    for ref, out, row in ((own, own_out, 0), (got, got_out, 4)):
        hot = ((slot == lane + plan[row, source]) & (lane < plan[row + 1, source])).astype(jnp.bfloat16)
        out[...] = jnp.dot(hot, ref[0], preferred_element_type=jnp.float32).astype(out.dtype)


def select(plan, cap, own, got):
    chips, size, cols = own.shape
    return pl.pallas_call(
        functools.partial(select_kernel, cap),
        grid_spec=pltpu.PrefetchScalarGridSpec(
            num_scalar_prefetch=1,
            grid=(chips,),
            in_specs=[pl.BlockSpec((1, size, cols), lambda s, _: (s, 0, 0))] * 2,
            out_specs=[pl.BlockSpec((cap, cols), lambda s, _: (s, 0))] * 2,
        ),
        out_shape=[jax.ShapeDtypeStruct((chips * cap, cols), jnp.bfloat16)] * 2,
        compiler_params=pltpu.CompilerParams(vmem_limit_bytes=VMEM),
        cost_estimate=NO_COST,
    )(plan, own, got)


def product_kernel(*refs):
    grad_a, grad_b, hidden_a, hidden_b, out = refs[-5:]
    wide = 512 if out.shape[1] % 512 == 0 else out.shape[1]
    over_rows = (((0,), (0,)), ((), ()))

    for n in range(0, out.shape[1], wide):
        at = slice(n, n + wide)
        half = lax.dot_general(grad_a[...], hidden_a[:, at], over_rows, preferred_element_type=jnp.float32)
        rest = lax.dot_general(grad_b[...], hidden_b[:, at], over_rows, preferred_element_type=jnp.float32)
        out[:, at] = (half + rest).astype(out.dtype)


def product_into(total, grads, hiddens, first, rows):
    depth, part = grads[0].shape
    wide = hiddens[0].shape[1]
    start = first // COLUMN
    held = [] if total is None else [total]
    return pl.pallas_call(
        product_kernel,
        grid=(part // COLUMN,),
        in_specs=[pl.BlockSpec(memory_space=pl.ANY)] * len(held)
        + [pl.BlockSpec((depth, COLUMN), lambda m: (0, m))] * 2
        + [pl.BlockSpec((depth, wide), lambda m: (0, 0))] * 2,
        out_specs=pl.BlockSpec((COLUMN, wide), lambda m: (m + start, 0)),
        out_shape=jax.ShapeDtypeStruct((rows, wide), jnp.bfloat16),
        input_output_aliases={0: 0} if held else {},
        compiler_params=pltpu.CompilerParams(vmem_limit_bytes=VMEM),
        cost_estimate=NO_COST,
    )(*held, *grads, *hiddens)


def per_device(hidden_rows, grad_rows, gate_prob, routes):
    row_count = routes.shape[0]
    dp_count = lax.axis_size("dp")
    chips = lax.axis_size("chip")
    experts = chips * CORES
    cap = 3 * row_count * dp_count // experts
    width = CORES * cap
    me_dp = lax.axis_index("dp")
    me_chip = lax.axis_index("chip")
    me_core = lax.axis_index("core")
    col_width = grad_rows.shape[1] // dp_count
    blocks = col_width // COLUMN
    cuts = (0, max(1, blocks - LAST) * COLUMN, col_width)

    route_group = jnp.stack(shifted(routes, "dp", dp_count))
    weighted = (gate_prob[:, None] * hidden_rows.astype(jnp.float32)).astype(jnp.bfloat16)
    hidden_group = spread_columns(weighted, dp_count)
    source = ((me_dp - jnp.arange(dp_count)) % dp_count).astype(jnp.int32)
    member = (route_group[:, :, None] == jnp.arange(experts, dtype=jnp.int32)).astype(jnp.float32)
    below = jnp.tril(jnp.ones((row_count, row_count), jnp.float32), -1)
    inside = jnp.einsum("qr,sre->sqe", below, member, preferred_element_type=jnp.float32)
    block_sum = jnp.sum(member, axis=1)
    before = jnp.einsum(
        "st,te->se", (source[None, :] < source[:, None]).astype(jnp.float32), block_sum
    )
    total = jnp.sum(block_sum, axis=0)
    pair_first = jnp.where(
        jnp.arange(experts) % CORES == 1, jnp.concatenate([jnp.zeros((1,), jnp.float32), total[:-1]]), 0.0
    )
    position = jnp.sum(member * (inside + before[:, None, :] + pair_first), axis=2)
    position = position.astype(jnp.int32).reshape(-1)
    to_chip = route_group.reshape(-1) // CORES

    both = jnp.stack(shifted(total.astype(jnp.int32), "core", CORES))
    counts = jnp.stack(shifted(both, "chip", chips))
    units = SIZES if chips <= ADAPTIVE_CHIPS else SIZES[-1:]
    sizes = [size * cap // UNITS for size in units]
    plan = make_plan(sizes, jnp.stack([me_chip, me_core]).astype(jnp.int32), counts)
    where = jnp.stack([to_chip, position])
    early = sizes[-2] if len(sizes) > 1 else sizes[-1]
    hidden_early = pack(where, chips, early, hidden_group)[0]

    def windows(blocks):
        own, other = unpack(plan, source, cap, blocks)
        return own, lax.ppermute(other, "core", [(a, (a + 1) % CORES) for a in range(CORES)])

    def branch(size):
        def run(hidden_early, hidden_group, grad_rows):
            if size <= early:
                hidden_own = hidden_early[:, :size]
            else:
                hidden_own = pack(where, chips, size, hidden_group)[0]
            hidden_own = exchange(hidden_own)
            grad_group = spread_columns(grad_rows, dp_count)
            grad_parts = [grad_group[:, low:high] for low, high in zip(cuts, cuts[1:])]
            packed = lax.optimization_barrier(pack(where, chips, size, *grad_parts))
            hidden_all = shifted(hidden_own, "dp", dp_count)
            parts = [exchange(part) for part in packed]
            hiddens = windows(hidden_all)
            total = None
            for low, part in zip(cuts, parts):
                if total is not None:
                    part, total = lax.optimization_barrier((part, total))
                got = lax.ppermute(part, "core", [(a, (a + 1) % CORES) for a in range(CORES)])
                total = product_into(total, select(plan, cap, part, got), hiddens, low, col_width)
            return total

        return run

    operands = (hidden_early, hidden_group, grad_rows)
    if len(sizes) == 1:
        return branch(sizes[0])(*operands)[None]
    return lax.switch(plan[6, 0], [branch(size) for size in sizes], *operands)[None]


def solution(mesh):
    dp_count, exp_count = mesh.shape["dp"], mesh.shape["expert"]
    fine = Mesh(mesh.devices.reshape(dp_count, exp_count // CORES, CORES), ("dp", "chip", "core"))
    rows = ("dp", "chip", "core")
    placed = (P(rows, None), P(rows, None), P(rows), P(rows))
    return jax.shard_map(
        per_device, mesh=fine, in_specs=placed, out_specs=P(("chip", "core"), "dp", None), check_vma=False
    )
```

```python
import functools

import jax
import jax.numpy as jnp
from jax import lax
from jax.experimental import pallas as pl
from jax.experimental.pallas import tpu as pltpu
from jax.sharding import Mesh, PartitionSpec as P

CORES = 2
ADAPTIVE_CHIPS = 4
UNITS = 12
SIZES = (13, 15, 17, 19, 20, 24)
COLUMN = 256
LAST = 2
VMEM = 28 * 2**20
NO_COST = pl.CostEstimate(flops=0, bytes_accessed=0, transcendentals=0)


def shifted(value, axis, count):
    return [value] + [
        lax.ppermute(value, axis, [(a, (a + s) % count) for a in range(count)]) for s in range(1, count)
    ]


def spread_columns(value, count):
    width = value.shape[1] // count
    me = lax.axis_index("dp")
    out = []
    for s in range(count):
        block = lax.dynamic_slice_in_dim(value, ((me + s) % count) * width, width, 1)
        if s:
            block = lax.ppermute(block, "dp", [(a, (a + s) % count) for a in range(count)])
        out.append(block)
    return jnp.concatenate(out, axis=0)


def pack_kernel(where, *refs):
    chip = pl.program_id(0)
    half = len(refs) // 2
    size = refs[-1].shape[1]
    slot = lax.broadcasted_iota(jnp.int32, (size, where.shape[1]), 0)
    onehot = ((where[1:2, :] == slot) & (where[0:1, :] == chip)).astype(jnp.bfloat16)
    for rows, out in zip(refs[:half], refs[half:]):
        out[0] = jnp.dot(onehot, rows[...], preferred_element_type=jnp.float32).astype(out.dtype)


def pack(where, chips, size, *values):
    count = values[0].shape[0]
    return pl.pallas_call(
        pack_kernel,
        grid=(chips,),
        in_specs=[pl.BlockSpec((2, count), lambda z: (0, 0))]
        + [pl.BlockSpec(v.shape, lambda z: (0, 0)) for v in values],
        out_specs=[pl.BlockSpec((1, size, v.shape[1]), lambda z: (z, 0, 0)) for v in values],
        out_shape=[jax.ShapeDtypeStruct((chips, size, v.shape[1]), jnp.bfloat16) for v in values],
        compiler_params=pltpu.CompilerParams(vmem_limit_bytes=VMEM),
        cost_estimate=pl.CostEstimate(
            flops=2 * chips * size * sum(v.size for v in values),
            bytes_accessed=2 * sum(v.size + chips * size * v.shape[1] for v in values),
            transcendentals=0,
        ),
    )(where, *values)


def exchange(blocks):
    return lax.all_to_all(blocks, "chip", split_axis=0, concat_axis=0, tiled=True)


def plan_kernel(sizes, place, counts, out):
    chips, cores, experts = counts.shape
    chip, core = place[0], place[1]
    for source in range(chips):
        back = lax.rem(chip - source + chips, chips)
        first = counts[back, 0, CORES * chip]
        second = counts[back, 0, CORES * chip + 1]
        out[0, source] = jnp.where(core == 0, 0, first)
        out[1, source] = jnp.where(core == 0, first, second)
        out[2, source] = jnp.where(core == 0, first, 0)
        out[3, source] = jnp.where(core == 0, second, first)
        first = counts[back, 1, CORES * chip]
        second = counts[back, 1, CORES * chip + 1]
        out[4, source] = jnp.where(core == 0, 0, first)
        out[5, source] = jnp.where(core == 0, first, second)
        out[6, source] = 0
    if len(sizes) == 1:
        return
    most = jnp.int32(0)
    for z in range(chips):
        for b in range(chips):
            for c in range(cores):
                most = jnp.maximum(most, counts[b, c, CORES * z] + counts[b, c, CORES * z + 1])
    which = jnp.int32(0)
    for size in sizes[:-1]:
        which += (most > size).astype(jnp.int32)
    out[6, 0] = which


def make_plan(sizes, place, counts):
    smem = pl.BlockSpec(memory_space=pltpu.SMEM)
    return pl.pallas_call(
        functools.partial(plan_kernel, sizes),
        in_specs=[smem, smem],
        out_specs=smem,
        out_shape=jax.ShapeDtypeStruct((7, counts.shape[0]), jnp.int32),
    )(place, counts)


def unpack_kernel(cap, plan, columns, *refs):
    refs, (own, other) = refs[:-2], refs[-2:]
    source = pl.program_id(0)
    wide = own.shape[1] // len(refs)
    shape = (2 * cap, refs[0].shape[1])
    lane = lax.broadcasted_iota(jnp.int32, shape, 0)
    slot = lax.broadcasted_iota(jnp.int32, shape, 1)
    top = lane < cap
    low = jnp.where(top, plan[0, source], plan[2, source] - cap)
    count = jnp.where(top, plan[1, source], plan[3, source] + cap)
    hot = ((slot == lane + low) & (lane < count)).astype(jnp.bfloat16)
    for g, ref in enumerate(refs):
        both = jnp.dot(hot, ref[0], preferred_element_type=jnp.float32).astype(own.dtype)
        at = pl.ds(pl.multiple_of(columns[g] * wide, wide) if len(refs) > 1 else 0, wide)
        own[:, at] = both[:cap]
        other[:, at] = both[cap:]


def unpack(plan, columns, cap, blocks):
    chips, _, wide = blocks[0].shape
    result = jax.ShapeDtypeStruct((chips * cap, wide * len(blocks)), jnp.bfloat16)
    return pl.pallas_call(
        functools.partial(unpack_kernel, cap),
        grid_spec=pltpu.PrefetchScalarGridSpec(
            num_scalar_prefetch=2,
            grid=(chips,),
            in_specs=[pl.BlockSpec((1,) + b.shape[1:], lambda s, *_: (s, 0, 0)) for b in blocks],
            out_specs=[pl.BlockSpec((cap, wide * len(blocks)), lambda s, *_: (s, 0))] * 2,
        ),
        out_shape=[result] * 2,
        compiler_params=pltpu.CompilerParams(vmem_limit_bytes=VMEM),
        cost_estimate=NO_COST,
    )(plan, columns, *blocks)


def select_kernel(cap, plan, own, got, own_out, got_out):
    source = pl.program_id(0)
    shape = (cap, own.shape[1])
    lane = lax.broadcasted_iota(jnp.int32, shape, 0)
    slot = lax.broadcasted_iota(jnp.int32, shape, 1)
    for ref, out, row in ((own, own_out, 0), (got, got_out, 4)):
        hot = ((slot == lane + plan[row, source]) & (lane < plan[row + 1, source])).astype(jnp.bfloat16)
        out[...] = jnp.dot(hot, ref[0], preferred_element_type=jnp.float32).astype(out.dtype)


def select(plan, cap, own, got):
    chips, size, cols = own.shape
    return pl.pallas_call(
        functools.partial(select_kernel, cap),
        grid_spec=pltpu.PrefetchScalarGridSpec(
            num_scalar_prefetch=1,
            grid=(chips,),
            in_specs=[pl.BlockSpec((1, size, cols), lambda s, _: (s, 0, 0))] * 2,
            out_specs=[pl.BlockSpec((cap, cols), lambda s, _: (s, 0))] * 2,
        ),
        out_shape=[jax.ShapeDtypeStruct((chips * cap, cols), jnp.bfloat16)] * 2,
        compiler_params=pltpu.CompilerParams(vmem_limit_bytes=VMEM),
        cost_estimate=NO_COST,
    )(plan, own, got)


def product_kernel(*refs):
    grad_a, grad_b, hidden_a, hidden_b, out = refs[-5:]
    wide = 512 if out.shape[1] % 512 == 0 else out.shape[1]
    over_rows = (((0,), (0,)), ((), ()))

    for n in range(0, out.shape[1], wide):
        at = slice(n, n + wide)
        half = lax.dot_general(grad_a[...], hidden_a[:, at], over_rows, preferred_element_type=jnp.float32)
        rest = lax.dot_general(grad_b[...], hidden_b[:, at], over_rows, preferred_element_type=jnp.float32)
        out[:, at] = (half + rest).astype(out.dtype)


def product_into(total, grads, hiddens, first, rows):
    depth, part = grads[0].shape
    wide = hiddens[0].shape[1]
    start = first // COLUMN
    held = [] if total is None else [total]
    return pl.pallas_call(
        product_kernel,
        grid=(part // COLUMN,),
        in_specs=[pl.BlockSpec(memory_space=pl.ANY)] * len(held)
        + [pl.BlockSpec((depth, COLUMN), lambda m: (0, m))] * 2
        + [pl.BlockSpec((depth, wide), lambda m: (0, 0))] * 2,
        out_specs=pl.BlockSpec((COLUMN, wide), lambda m: (m + start, 0)),
        out_shape=jax.ShapeDtypeStruct((rows, wide), jnp.bfloat16),
        input_output_aliases={0: 0} if held else {},
        compiler_params=pltpu.CompilerParams(vmem_limit_bytes=VMEM),
        cost_estimate=NO_COST,
    )(*held, *grads, *hiddens)


def per_device(hidden_rows, grad_rows, gate_prob, routes):
    row_count = routes.shape[0]
    dp_count = lax.axis_size("dp")
    chips = lax.axis_size("chip")
    experts = chips * CORES
    cap = 3 * row_count * dp_count // experts
    width = CORES * cap
    me_dp = lax.axis_index("dp")
    me_chip = lax.axis_index("chip")
    me_core = lax.axis_index("core")
    col_width = grad_rows.shape[1] // dp_count
    blocks = col_width // COLUMN
    cuts = (0, max(1, blocks - LAST) * COLUMN, col_width)

    route_group = jnp.stack(shifted(routes, "dp", dp_count))
    weighted = (gate_prob[:, None] * hidden_rows.astype(jnp.float32)).astype(jnp.bfloat16)
    hidden_group = spread_columns(weighted, dp_count)
    source = ((me_dp - jnp.arange(dp_count)) % dp_count).astype(jnp.int32)
    member = (route_group[:, :, None] == jnp.arange(experts, dtype=jnp.int32)).astype(jnp.float32)
    below = jnp.tril(jnp.ones((row_count, row_count), jnp.float32), -1)
    inside = jnp.einsum("qr,sre->sqe", below, member, preferred_element_type=jnp.float32)
    block_sum = jnp.sum(member, axis=1)
    before = jnp.einsum(
        "st,te->se", (source[None, :] < source[:, None]).astype(jnp.float32), block_sum
    )
    total = jnp.sum(block_sum, axis=0)
    pair_first = jnp.where(
        jnp.arange(experts) % CORES == 1, jnp.concatenate([jnp.zeros((1,), jnp.float32), total[:-1]]), 0.0
    )
    position = jnp.sum(member * (inside + before[:, None, :] + pair_first), axis=2)
    position = position.astype(jnp.int32).reshape(-1)
    to_chip = route_group.reshape(-1) // CORES

    both = jnp.stack(shifted(total.astype(jnp.int32), "core", CORES))
    counts = jnp.stack(shifted(both, "chip", chips))
    units = SIZES if chips <= ADAPTIVE_CHIPS else SIZES[-1:]
    sizes = [size * cap // UNITS for size in units]
    plan = make_plan(sizes, jnp.stack([me_chip, me_core]).astype(jnp.int32), counts)
    where = jnp.stack([to_chip, position])
    early = sizes[-2] if len(sizes) > 1 else sizes[-1]
    hidden_early = pack(where, chips, early, hidden_group)[0]

    def windows(blocks):
        own, other = unpack(plan, source, cap, blocks)
        return own, lax.ppermute(other, "core", [(a, (a + 1) % CORES) for a in range(CORES)])

    def branch(size):
        def run(hidden_early, hidden_group, grad_rows):
            if size <= early:
                hidden_own = hidden_early[:, :size]
            else:
                hidden_own = pack(where, chips, size, hidden_group)[0]
            hidden_own = exchange(hidden_own)
            grad_group = spread_columns(grad_rows, dp_count)
            grad_parts = [grad_group[:, low:high] for low, high in zip(cuts, cuts[1:])]
            packed = lax.optimization_barrier(pack(where, chips, size, *grad_parts))
            hidden_all = shifted(hidden_own, "dp", dp_count)
            parts = [exchange(part) for part in packed]
            hiddens = windows(hidden_all)
            total = None
            for low, part in zip(cuts, parts):
                if total is not None:
                    part, total = lax.optimization_barrier((part, total))
                got = lax.ppermute(part, "core", [(a, (a + 1) % CORES) for a in range(CORES)])
                total = product_into(total, select(plan, cap, part, got), hiddens, low, col_width)
            return total

        return run

    operands = (hidden_early, hidden_group, grad_rows)
    if len(sizes) == 1:
        return branch(sizes[0])(*operands)[None]
    return lax.switch(plan[6, 0], [branch(size) for size in sizes], *operands)[None]


def solution(mesh):
    dp_count, exp_count = mesh.shape["dp"], mesh.shape["expert"]
    fine = Mesh(mesh.devices.reshape(dp_count, exp_count // CORES, CORES), ("dp", "chip", "core"))
    rows = ("dp", "chip", "core")
    placed = (P(rows, None), P(rows, None), P(rows), P(rows))
    return jax.shard_map(
        per_device, mesh=fine, in_specs=placed, out_specs=P(("chip", "core"), "dp", None), check_vma=False
    )
```

```python
import functools

import jax
import jax.numpy as jnp
from jax import lax
from jax.experimental import pallas as pl
from jax.experimental.pallas import tpu as pltpu
from jax.sharding import Mesh, PartitionSpec as P

CORES = 2
ADAPTIVE_CHIPS = 4
UNITS = 12
SIZES = (13, 15, 17, 19, 20, 24)
COLUMN = 256
LAST = 2
VMEM = 28 * 2**20
NO_COST = pl.CostEstimate(flops=0, bytes_accessed=0, transcendentals=0)


def shifted(value, axis, count):
    return [value] + [
        lax.ppermute(value, axis, [(a, (a + s) % count) for a in range(count)]) for s in range(1, count)
    ]


def spread_columns(value, count):
    width = value.shape[1] // count
    me = lax.axis_index("dp")
    out = []
    for s in range(count):
        block = lax.dynamic_slice_in_dim(value, ((me + s) % count) * width, width, 1)
        if s:
            block = lax.ppermute(block, "dp", [(a, (a + s) % count) for a in range(count)])
        out.append(block)
    return jnp.concatenate(out, axis=0)


def pack_kernel(where, *refs):
    chip = pl.program_id(0)
    half = len(refs) // 2
    size = refs[-1].shape[1]
    slot = lax.broadcasted_iota(jnp.int32, (size, where.shape[1]), 0)
    onehot = ((where[1:2, :] == slot) & (where[0:1, :] == chip)).astype(jnp.bfloat16)
    for rows, out in zip(refs[:half], refs[half:]):
        out[0] = jnp.dot(onehot, rows[...], preferred_element_type=jnp.float32).astype(out.dtype)


def pack(where, chips, size, *values):
    count = values[0].shape[0]
    return pl.pallas_call(
        pack_kernel,
        grid=(chips,),
        in_specs=[pl.BlockSpec((2, count), lambda z: (0, 0))]
        + [pl.BlockSpec(v.shape, lambda z: (0, 0)) for v in values],
        out_specs=[pl.BlockSpec((1, size, v.shape[1]), lambda z: (z, 0, 0)) for v in values],
        out_shape=[jax.ShapeDtypeStruct((chips, size, v.shape[1]), jnp.bfloat16) for v in values],
        compiler_params=pltpu.CompilerParams(vmem_limit_bytes=VMEM),
        cost_estimate=pl.CostEstimate(
            flops=2 * chips * size * sum(v.size for v in values),
            bytes_accessed=2 * sum(v.size + chips * size * v.shape[1] for v in values),
            transcendentals=0,
        ),
    )(where, *values)


def exchange(blocks):
    return lax.all_to_all(blocks, "chip", split_axis=0, concat_axis=0, tiled=True)


def plan_kernel(sizes, place, counts, out):
    chips, cores, experts = counts.shape
    chip, core = place[0], place[1]
    for source in range(chips):
        back = lax.rem(chip - source + chips, chips)
        first = counts[back, 0, CORES * chip]
        second = counts[back, 0, CORES * chip + 1]
        out[0, source] = jnp.where(core == 0, 0, first)
        out[1, source] = jnp.where(core == 0, first, second)
        out[2, source] = jnp.where(core == 0, first, 0)
        out[3, source] = jnp.where(core == 0, second, first)
        first = counts[back, 1, CORES * chip]
        second = counts[back, 1, CORES * chip + 1]
        out[4, source] = jnp.where(core == 0, 0, first)
        out[5, source] = jnp.where(core == 0, first, second)
        out[6, source] = 0
    if len(sizes) == 1:
        return
    most = jnp.int32(0)
    for z in range(chips):
        for b in range(chips):
            for c in range(cores):
                most = jnp.maximum(most, counts[b, c, CORES * z] + counts[b, c, CORES * z + 1])
    which = jnp.int32(0)
    for size in sizes[:-1]:
        which += (most > size).astype(jnp.int32)
    out[6, 0] = which


def make_plan(sizes, place, counts):
    smem = pl.BlockSpec(memory_space=pltpu.SMEM)
    return pl.pallas_call(
        functools.partial(plan_kernel, sizes),
        in_specs=[smem, smem],
        out_specs=smem,
        out_shape=jax.ShapeDtypeStruct((7, counts.shape[0]), jnp.int32),
    )(place, counts)


def unpack_kernel(cap, plan, columns, *refs):
    refs, (own, other) = refs[:-2], refs[-2:]
    source = pl.program_id(0)
    wide = own.shape[1] // len(refs)
    shape = (2 * cap, refs[0].shape[1])
    lane = lax.broadcasted_iota(jnp.int32, shape, 0)
    slot = lax.broadcasted_iota(jnp.int32, shape, 1)
    top = lane < cap
    low = jnp.where(top, plan[0, source], plan[2, source] - cap)
    count = jnp.where(top, plan[1, source], plan[3, source] + cap)
    hot = ((slot == lane + low) & (lane < count)).astype(jnp.bfloat16)
    for g, ref in enumerate(refs):
        both = jnp.dot(hot, ref[0], preferred_element_type=jnp.float32).astype(own.dtype)
        at = pl.ds(pl.multiple_of(columns[g] * wide, wide) if len(refs) > 1 else 0, wide)
        own[:, at] = both[:cap]
        other[:, at] = both[cap:]


def unpack(plan, columns, cap, blocks):
    chips, _, wide = blocks[0].shape
    result = jax.ShapeDtypeStruct((chips * cap, wide * len(blocks)), jnp.bfloat16)
    return pl.pallas_call(
        functools.partial(unpack_kernel, cap),
        grid_spec=pltpu.PrefetchScalarGridSpec(
            num_scalar_prefetch=2,
            grid=(chips,),
            in_specs=[pl.BlockSpec((1,) + b.shape[1:], lambda s, *_: (s, 0, 0)) for b in blocks],
            out_specs=[pl.BlockSpec((cap, wide * len(blocks)), lambda s, *_: (s, 0))] * 2,
        ),
        out_shape=[result] * 2,
        compiler_params=pltpu.CompilerParams(vmem_limit_bytes=VMEM),
        cost_estimate=NO_COST,
    )(plan, columns, *blocks)


def select_kernel(cap, plan, own, got, own_out, got_out):
    source = pl.program_id(0)
    shape = (cap, own.shape[1])
    lane = lax.broadcasted_iota(jnp.int32, shape, 0)
    slot = lax.broadcasted_iota(jnp.int32, shape, 1)
    for ref, out, row in ((own, own_out, 0), (got, got_out, 4)):
        hot = ((slot == lane + plan[row, source]) & (lane < plan[row + 1, source])).astype(jnp.bfloat16)
        out[...] = jnp.dot(hot, ref[0], preferred_element_type=jnp.float32).astype(out.dtype)


def select(plan, cap, own, got):
    chips, size, cols = own.shape
    return pl.pallas_call(
        functools.partial(select_kernel, cap),
        grid_spec=pltpu.PrefetchScalarGridSpec(
            num_scalar_prefetch=1,
            grid=(chips,),
            in_specs=[pl.BlockSpec((1, size, cols), lambda s, _: (s, 0, 0))] * 2,
            out_specs=[pl.BlockSpec((cap, cols), lambda s, _: (s, 0))] * 2,
        ),
        out_shape=[jax.ShapeDtypeStruct((chips * cap, cols), jnp.bfloat16)] * 2,
        compiler_params=pltpu.CompilerParams(vmem_limit_bytes=VMEM),
        cost_estimate=NO_COST,
    )(plan, own, got)


def product_kernel(*refs):
    grad_a, grad_b, hidden_a, hidden_b, out = refs[-5:]
    wide = 512 if out.shape[1] % 512 == 0 else out.shape[1]
    over_rows = (((0,), (0,)), ((), ()))

    for n in range(0, out.shape[1], wide):
        at = slice(n, n + wide)
        half = lax.dot_general(grad_a[...], hidden_a[:, at], over_rows, preferred_element_type=jnp.float32)
        rest = lax.dot_general(grad_b[...], hidden_b[:, at], over_rows, preferred_element_type=jnp.float32)
        out[:, at] = (half + rest).astype(out.dtype)


def product_into(total, grads, hiddens, first, rows):
    depth, part = grads[0].shape
    wide = hiddens[0].shape[1]
    start = first // COLUMN
    held = [] if total is None else [total]
    return pl.pallas_call(
        product_kernel,
        grid=(part // COLUMN,),
        in_specs=[pl.BlockSpec(memory_space=pl.ANY)] * len(held)
        + [pl.BlockSpec((depth, COLUMN), lambda m: (0, m))] * 2
        + [pl.BlockSpec((depth, wide), lambda m: (0, 0))] * 2,
        out_specs=pl.BlockSpec((COLUMN, wide), lambda m: (m + start, 0)),
        out_shape=jax.ShapeDtypeStruct((rows, wide), jnp.bfloat16),
        input_output_aliases={0: 0} if held else {},
        compiler_params=pltpu.CompilerParams(vmem_limit_bytes=VMEM),
        cost_estimate=NO_COST,
    )(*held, *grads, *hiddens)


def per_device(hidden_rows, grad_rows, gate_prob, routes):
    row_count = routes.shape[0]
    dp_count = lax.axis_size("dp")
    chips = lax.axis_size("chip")
    experts = chips * CORES
    cap = 3 * row_count * dp_count // experts
    width = CORES * cap
    me_dp = lax.axis_index("dp")
    me_chip = lax.axis_index("chip")
    me_core = lax.axis_index("core")
    col_width = grad_rows.shape[1] // dp_count
    blocks = col_width // COLUMN
    cuts = (0, max(1, blocks - LAST) * COLUMN, col_width)

    route_group = jnp.stack(shifted(routes, "dp", dp_count))
    weighted = (gate_prob[:, None] * hidden_rows.astype(jnp.float32)).astype(jnp.bfloat16)
    hidden_group = spread_columns(weighted, dp_count)
    source = ((me_dp - jnp.arange(dp_count)) % dp_count).astype(jnp.int32)
    member = (route_group[:, :, None] == jnp.arange(experts, dtype=jnp.int32)).astype(jnp.float32)
    below = jnp.tril(jnp.ones((row_count, row_count), jnp.float32), -1)
    inside = jnp.einsum("qr,sre->sqe", below, member, preferred_element_type=jnp.float32)
    block_sum = jnp.sum(member, axis=1)
    before = jnp.einsum(
        "st,te->se", (source[None, :] < source[:, None]).astype(jnp.float32), block_sum
    )
    total = jnp.sum(block_sum, axis=0)
    pair_first = jnp.where(
        jnp.arange(experts) % CORES == 1, jnp.concatenate([jnp.zeros((1,), jnp.float32), total[:-1]]), 0.0
    )
    position = jnp.sum(member * (inside + before[:, None, :] + pair_first), axis=2)
    position = position.astype(jnp.int32).reshape(-1)
    to_chip = route_group.reshape(-1) // CORES

    both = jnp.stack(shifted(total.astype(jnp.int32), "core", CORES))
    counts = jnp.stack(shifted(both, "chip", chips))
    units = SIZES if chips <= ADAPTIVE_CHIPS else SIZES[-1:]
    sizes = [size * cap // UNITS for size in units]
    plan = make_plan(sizes, jnp.stack([me_chip, me_core]).astype(jnp.int32), counts)
    where = jnp.stack([to_chip, position])
    early = sizes[-2] if len(sizes) > 1 else sizes[-1]
    hidden_early = pack(where, chips, early, hidden_group)[0]

    def windows(blocks):
        own, other = unpack(plan, source, cap, blocks)
        return own, lax.ppermute(other, "core", [(a, (a + 1) % CORES) for a in range(CORES)])

    def branch(size):
        def run(hidden_early, hidden_group, grad_rows):
            if size <= early:
                hidden_own = hidden_early[:, :size]
            else:
                hidden_own = pack(where, chips, size, hidden_group)[0]
            hidden_own = exchange(hidden_own)
            grad_group = spread_columns(grad_rows, dp_count)
            grad_parts = [grad_group[:, low:high] for low, high in zip(cuts, cuts[1:])]
            hidden_all = shifted(hidden_own, "dp", dp_count)
            first = exchange(pack(where, chips, size, grad_parts[0])[0])
            hidden_all, last = lax.optimization_barrier((hidden_all, grad_parts[1]))
            hidden_all, last = lax.optimization_barrier((hidden_all, pack(where, chips, size, last)[0]))
            parts = [first, exchange(last)]
            hiddens = windows(hidden_all)
            total = None
            for low, part in zip(cuts, parts):
                if total is not None:
                    part, total = lax.optimization_barrier((part, total))
                got = lax.ppermute(part, "core", [(a, (a + 1) % CORES) for a in range(CORES)])
                total = product_into(total, select(plan, cap, part, got), hiddens, low, col_width)
            return total

        return run

    operands = (hidden_early, hidden_group, grad_rows)
    if len(sizes) == 1:
        return branch(sizes[0])(*operands)[None]
    return lax.switch(plan[6, 0], [branch(size) for size in sizes], *operands)[None]


def solution(mesh):
    dp_count, exp_count = mesh.shape["dp"], mesh.shape["expert"]
    fine = Mesh(mesh.devices.reshape(dp_count, exp_count // CORES, CORES), ("dp", "chip", "core"))
    rows = ("dp", "chip", "core")
    placed = (P(rows, None), P(rows, None), P(rows), P(rows))
    return jax.shard_map(
        per_device, mesh=fine, in_specs=placed, out_specs=P(("chip", "core"), "dp", None), check_vma=False
    )
```

```python
import functools

import jax
import jax.numpy as jnp
from jax import lax
from jax.experimental import pallas as pl
from jax.experimental.pallas import tpu as pltpu
from jax.sharding import Mesh, PartitionSpec as P

CORES = 2
ADAPTIVE_CHIPS = 4
UNITS = 12
SIZES = (13, 15, 17, 19, 20, 24)
COLUMN = 256
LAST = 2
VMEM = 28 * 2**20
NO_COST = pl.CostEstimate(flops=0, bytes_accessed=0, transcendentals=0)


def shifted(value, axis, count):
    return [value] + [
        lax.ppermute(value, axis, [(a, (a + s) % count) for a in range(count)]) for s in range(1, count)
    ]


def spread_columns(value, count):
    width = value.shape[1] // count
    me = lax.axis_index("dp")
    out = []
    for s in range(count):
        block = lax.dynamic_slice_in_dim(value, ((me + s) % count) * width, width, 1)
        if s:
            block = lax.ppermute(block, "dp", [(a, (a + s) % count) for a in range(count)])
        out.append(block)
    return jnp.concatenate(out, axis=0)


def pack_kernel(where, *refs):
    chip = pl.program_id(0)
    half = len(refs) // 2
    size = refs[-1].shape[1]
    slot = lax.broadcasted_iota(jnp.int32, (size, where.shape[1]), 0)
    onehot = ((where[1:2, :] == slot) & (where[0:1, :] == chip)).astype(jnp.bfloat16)
    for rows, out in zip(refs[:half], refs[half:]):
        out[0] = jnp.dot(onehot, rows[...], preferred_element_type=jnp.float32).astype(out.dtype)


def pack(where, chips, size, *values):
    count = values[0].shape[0]
    return pl.pallas_call(
        pack_kernel,
        grid=(chips,),
        in_specs=[pl.BlockSpec((2, count), lambda z: (0, 0))]
        + [pl.BlockSpec(v.shape, lambda z: (0, 0)) for v in values],
        out_specs=[pl.BlockSpec((1, size, v.shape[1]), lambda z: (z, 0, 0)) for v in values],
        out_shape=[jax.ShapeDtypeStruct((chips, size, v.shape[1]), jnp.bfloat16) for v in values],
        compiler_params=pltpu.CompilerParams(vmem_limit_bytes=VMEM),
        cost_estimate=pl.CostEstimate(
            flops=2 * chips * size * sum(v.size for v in values),
            bytes_accessed=2 * sum(v.size + chips * size * v.shape[1] for v in values),
            transcendentals=0,
        ),
    )(where, *values)


def exchange(blocks):
    return lax.all_to_all(blocks, "chip", split_axis=0, concat_axis=0, tiled=True)


def plan_kernel(sizes, place, counts, out):
    chips, cores, experts = counts.shape
    chip, core = place[0], place[1]
    for source in range(chips):
        back = lax.rem(chip - source + chips, chips)
        first = counts[back, 0, CORES * chip]
        second = counts[back, 0, CORES * chip + 1]
        out[0, source] = jnp.where(core == 0, 0, first)
        out[1, source] = jnp.where(core == 0, first, second)
        out[2, source] = jnp.where(core == 0, first, 0)
        out[3, source] = jnp.where(core == 0, second, first)
        first = counts[back, 1, CORES * chip]
        second = counts[back, 1, CORES * chip + 1]
        out[4, source] = jnp.where(core == 0, 0, first)
        out[5, source] = jnp.where(core == 0, first, second)
        out[6, source] = 0
    if len(sizes) == 1:
        return
    most = jnp.int32(0)
    for z in range(chips):
        for b in range(chips):
            for c in range(cores):
                most = jnp.maximum(most, counts[b, c, CORES * z] + counts[b, c, CORES * z + 1])
    which = jnp.int32(0)
    for size in sizes[:-1]:
        which += (most > size).astype(jnp.int32)
    out[6, 0] = which


def make_plan(sizes, place, counts):
    smem = pl.BlockSpec(memory_space=pltpu.SMEM)
    return pl.pallas_call(
        functools.partial(plan_kernel, sizes),
        in_specs=[smem, smem],
        out_specs=smem,
        out_shape=jax.ShapeDtypeStruct((7, counts.shape[0]), jnp.int32),
    )(place, counts)


def unpack_kernel(cap, plan, columns, *refs):
    refs, (own, other) = refs[:-2], refs[-2:]
    source = pl.program_id(0)
    wide = own.shape[1] // len(refs)
    shape = (2 * cap, refs[0].shape[1])
    lane = lax.broadcasted_iota(jnp.int32, shape, 0)
    slot = lax.broadcasted_iota(jnp.int32, shape, 1)
    top = lane < cap
    low = jnp.where(top, plan[0, source], plan[2, source] - cap)
    count = jnp.where(top, plan[1, source], plan[3, source] + cap)
    hot = ((slot == lane + low) & (lane < count)).astype(jnp.bfloat16)
    for g, ref in enumerate(refs):
        both = jnp.dot(hot, ref[0], preferred_element_type=jnp.float32).astype(own.dtype)
        at = pl.ds(pl.multiple_of(columns[g] * wide, wide) if len(refs) > 1 else 0, wide)
        own[:, at] = both[:cap]
        other[:, at] = both[cap:]


def unpack(plan, columns, cap, blocks):
    chips, _, wide = blocks[0].shape
    result = jax.ShapeDtypeStruct((chips * cap, wide * len(blocks)), jnp.bfloat16)
    return pl.pallas_call(
        functools.partial(unpack_kernel, cap),
        grid_spec=pltpu.PrefetchScalarGridSpec(
            num_scalar_prefetch=2,
            grid=(chips,),
            in_specs=[pl.BlockSpec((1,) + b.shape[1:], lambda s, *_: (s, 0, 0)) for b in blocks],
            out_specs=[pl.BlockSpec((cap, wide * len(blocks)), lambda s, *_: (s, 0))] * 2,
        ),
        out_shape=[result] * 2,
        compiler_params=pltpu.CompilerParams(vmem_limit_bytes=VMEM),
        cost_estimate=NO_COST,
    )(plan, columns, *blocks)


def select_kernel(cap, plan, own, got, own_out, got_out):
    source = pl.program_id(0)
    shape = (cap, own.shape[1])
    lane = lax.broadcasted_iota(jnp.int32, shape, 0)
    slot = lax.broadcasted_iota(jnp.int32, shape, 1)
    for ref, out, row in ((own, own_out, 0), (got, got_out, 4)):
        hot = ((slot == lane + plan[row, source]) & (lane < plan[row + 1, source])).astype(jnp.bfloat16)
        out[...] = jnp.dot(hot, ref[0], preferred_element_type=jnp.float32).astype(out.dtype)


def select(plan, cap, own, got):
    chips, size, cols = own.shape
    return pl.pallas_call(
        functools.partial(select_kernel, cap),
        grid_spec=pltpu.PrefetchScalarGridSpec(
            num_scalar_prefetch=1,
            grid=(chips,),
            in_specs=[pl.BlockSpec((1, size, cols), lambda s, _: (s, 0, 0))] * 2,
            out_specs=[pl.BlockSpec((cap, cols), lambda s, _: (s, 0))] * 2,
        ),
        out_shape=[jax.ShapeDtypeStruct((chips * cap, cols), jnp.bfloat16)] * 2,
        compiler_params=pltpu.CompilerParams(vmem_limit_bytes=VMEM),
        cost_estimate=NO_COST,
    )(plan, own, got)


def product_kernel(*refs):
    grad_a, grad_b, hidden_a, hidden_b, out = refs[-5:]
    wide = 512 if out.shape[1] % 512 == 0 else out.shape[1]
    over_rows = (((0,), (0,)), ((), ()))

    for n in range(0, out.shape[1], wide):
        at = slice(n, n + wide)
        half = lax.dot_general(grad_a[...], hidden_a[:, at], over_rows, preferred_element_type=jnp.float32)
        rest = lax.dot_general(grad_b[...], hidden_b[:, at], over_rows, preferred_element_type=jnp.float32)
        out[:, at] = (half + rest).astype(out.dtype)


def product_into(total, grads, hiddens, first, rows):
    depth, part = grads[0].shape
    wide = hiddens[0].shape[1]
    start = first // COLUMN
    held = [] if total is None else [total]
    return pl.pallas_call(
        product_kernel,
        grid=(part // COLUMN,),
        in_specs=[pl.BlockSpec(memory_space=pl.ANY)] * len(held)
        + [pl.BlockSpec((depth, COLUMN), lambda m: (0, m))] * 2
        + [pl.BlockSpec((depth, wide), lambda m: (0, 0))] * 2,
        out_specs=pl.BlockSpec((COLUMN, wide), lambda m: (m + start, 0)),
        out_shape=jax.ShapeDtypeStruct((rows, wide), jnp.bfloat16),
        input_output_aliases={0: 0} if held else {},
        compiler_params=pltpu.CompilerParams(vmem_limit_bytes=VMEM),
        cost_estimate=NO_COST,
    )(*held, *grads, *hiddens)


def per_device(hidden_rows, grad_rows, gate_prob, routes):
    row_count = routes.shape[0]
    dp_count = lax.axis_size("dp")
    chips = lax.axis_size("chip")
    experts = chips * CORES
    cap = 3 * row_count * dp_count // experts
    width = CORES * cap
    me_dp = lax.axis_index("dp")
    me_chip = lax.axis_index("chip")
    me_core = lax.axis_index("core")
    col_width = grad_rows.shape[1] // dp_count
    blocks = col_width // COLUMN
    cuts = (0, max(1, blocks - LAST) * COLUMN, col_width)

    route_group = jnp.stack(shifted(routes, "dp", dp_count))
    weighted = (gate_prob[:, None] * hidden_rows.astype(jnp.float32)).astype(jnp.bfloat16)
    hidden_group = spread_columns(weighted, dp_count)
    source = ((me_dp - jnp.arange(dp_count)) % dp_count).astype(jnp.int32)
    member = (route_group[:, :, None] == jnp.arange(experts, dtype=jnp.int32)).astype(jnp.float32)
    below = jnp.tril(jnp.ones((row_count, row_count), jnp.float32), -1)
    inside = jnp.einsum("qr,sre->sqe", below, member, preferred_element_type=jnp.float32)
    block_sum = jnp.sum(member, axis=1)
    before = jnp.einsum(
        "st,te->se", (source[None, :] < source[:, None]).astype(jnp.float32), block_sum
    )
    total = jnp.sum(block_sum, axis=0)
    pair_first = jnp.where(
        jnp.arange(experts) % CORES == 1, jnp.concatenate([jnp.zeros((1,), jnp.float32), total[:-1]]), 0.0
    )
    position = jnp.sum(member * (inside + before[:, None, :] + pair_first), axis=2)
    position = position.astype(jnp.int32).reshape(-1)
    to_chip = route_group.reshape(-1) // CORES

    both = jnp.stack(shifted(total.astype(jnp.int32), "core", CORES))
    counts = jnp.stack(shifted(both, "chip", chips))
    units = SIZES if chips <= ADAPTIVE_CHIPS else SIZES[-1:]
    sizes = [size * cap // UNITS for size in units]
    plan = make_plan(sizes, jnp.stack([me_chip, me_core]).astype(jnp.int32), counts)
    where = jnp.stack([to_chip, position])
    def windows(blocks):
        own, other = unpack(plan, source, cap, blocks)
        return own, lax.ppermute(other, "core", [(a, (a + 1) % CORES) for a in range(CORES)])

    def branch(size):
        def run(hidden_group, grad_rows):
            hidden_own = pack(where, chips, size, hidden_group)[0]
            hidden_own = exchange(hidden_own)
            grad_group = spread_columns(grad_rows, dp_count)
            grad_parts = [grad_group[:, low:high] for low, high in zip(cuts, cuts[1:])]
            hidden_all = shifted(hidden_own, "dp", dp_count)
            first = exchange(pack(where, chips, size, grad_parts[0])[0])
            hidden_all, last = lax.optimization_barrier((hidden_all, grad_parts[1]))
            hidden_all, last = lax.optimization_barrier((hidden_all, pack(where, chips, size, last)[0]))
            parts = [first, exchange(last)]
            hiddens = windows(hidden_all)
            total = None
            for low, part in zip(cuts, parts):
                if total is not None:
                    part, total = lax.optimization_barrier((part, total))
                got = lax.ppermute(part, "core", [(a, (a + 1) % CORES) for a in range(CORES)])
                total = product_into(total, select(plan, cap, part, got), hiddens, low, col_width)
            return total

        return run

    operands = (hidden_group, grad_rows)
    if len(sizes) == 1:
        return branch(sizes[0])(*operands)[None]
    return lax.switch(plan[6, 0], [branch(size) for size in sizes], *operands)[None]


def solution(mesh):
    dp_count, exp_count = mesh.shape["dp"], mesh.shape["expert"]
    fine = Mesh(mesh.devices.reshape(dp_count, exp_count // CORES, CORES), ("dp", "chip", "core"))
    rows = ("dp", "chip", "core")
    placed = (P(rows, None), P(rows, None), P(rows), P(rows))
    return jax.shard_map(
        per_device, mesh=fine, in_specs=placed, out_specs=P(("chip", "core"), "dp", None), check_vma=False
    )
```
